512 devices in a mesh: energy: 128 (over y_hi, z, x), slab: 4 (over y_lo, core).
Axes of the slice: x: 4, y: 8 (y_hi: 4, y_lo: 2; y = y_hi * 2 + y_lo), z: 8, core: 2. Of those that a mesh axis runs over, the one named last changes fastest.
Arguments:
- green_blocks: bfloat16 [128, 4, 512, 512], P('energy', 'slab'), may hold values from -6 to 6
- coulomb: bfloat16 [4, 512, 512], P('slab'), may hold values from -0.25 to 0.25
- couple_cols: int32 [4, 128, 8], P('slab'), may hold values from 0 to 127
- couple_vals: bfloat16 [4, 128, 8], P('slab'), may hold values from -0.8984375 to 0.8984375
Outputs:
- new_green: bfloat16 [128, 4, 512, 512], P('energy', 'slab')
The draws below stay inside these ranges and needn't reach their ends.
Inputs may be any that keep to these rules, and one draw needn't show every extreme that they name: couple_cols[s, i, k] names one of the first 128 orbitals of slab s + 1.
All inputs are finite; a program needn't handle non-finite values.
Results may differ from the reference program's by a relative error of at most 0.015.
Values may be sent and summed in bfloat16 or wider, within the bound.
No kernel may reach another device: no remote copies, remote signals or barrier semaphores. Data moves between devices by JAX's collectives and lax.ppermute only.
A program may use at most 64 MiB of HBM per device.

```python
import math
import jax
import jax.numpy as jnp
from jax import lax

M = 512
COUPLINGS = 8
IFACE = 128
NE = 128
SLABS = 4


def with_ends(values, own_key, least, high):
    spot = [jax.random.randint(jax.random.fold_in(own_key, axis), (), 0, length) for axis, length in enumerate(values.shape)]
    main_axis = values.shape.index(max(values.shape))
    neighbour = spot[:main_axis] + [(spot[main_axis] + 1) % values.shape[main_axis]] + spot[main_axis + 1:]
    return values.at[tuple(spot)].set(least).at[tuple(neighbour)].set(high)


def block_scale(own_key, dims, split, low, largest):
    factor_of = 1.0
    for position, shards_of in split:
        steps = jax.random.uniform(jax.random.fold_in(jax.random.fold_in(own_key, 6), position), (shards_of,), jnp.float32, low / len(split), largest / len(split))
        factor_of = factor_of * jnp.repeat(jnp.exp(steps), dims[position] // shards_of).reshape((-1,) + (1,) * (len(dims) - 1 - position))
    return factor_of


def bell_draw(rng, shape, deviation, bound, cuts=(), kind=jnp.bfloat16):
    array = jax.random.normal(rng, shape, jnp.float32) * deviation
    if len(cuts) > 0:
        array = block_scale(rng, shape, cuts, -0.22, 0.18) * array
    return jnp.clip(array, min=-bound, max=bound).astype(kind)


def setup_inputs(seed: int = 0) -> dict:
    streams_of = jax.random.split(jax.random.key(seed), 5)
    green_blocks = bell_draw(streams_of[0], (NE, SLABS, M, M), 1.0, 6.0, ((0, 128), (1, 4)))
    coulomb = bell_draw(streams_of[1], (SLABS, M, M), M ** -0.5, 0.25, ((0, 4),))
    couple_cols = with_ends(jax.random.randint(streams_of[2], (SLABS, IFACE, COUPLINGS), 0, IFACE), jax.random.fold_in(streams_of[2], 1), 0, IFACE - 1).astype(jnp.int32)
    couple_vals = bell_draw(streams_of[3], (SLABS, IFACE, COUPLINGS), 0.15, 0.8984375, ((0, 4),))
    return dict(green_blocks=green_blocks, coulomb=coulomb, couple_cols=couple_cols, couple_vals=couple_vals)


row_block = 32

def coupling_matrix(column_ids, coupling_values):
    width = column_ids.shape[0]
    hits = column_ids[:, :, None] == jnp.arange(width, dtype=jnp.int32)[None, None, :]
    summed = lax.optimization_barrier(jnp.sum(jnp.where(hits, coupling_values.astype(jnp.float32)[:, :, None], jnp.float32(0.0)), axis=1))
    return summed.astype(jnp.bfloat16)

def screen(polar_one, coulomb_block):
    inner = jnp.dot(coulomb_block, polar_one, preferred_element_type=jnp.float32).astype(jnp.bfloat16)
    second = jnp.dot(inner, coulomb_block, preferred_element_type=jnp.float32)
    third = jnp.dot(inner, second.astype(jnp.bfloat16), preferred_element_type=jnp.float32)
    return (coulomb_block.astype(jnp.float32) + second + third).astype(jnp.bfloat16)

def batched(left, right):
    return jnp.einsum('eij,ejk->eik', left.astype(jnp.float32), right.astype(jnp.float32))

def reference(green_blocks, coulomb, couple_cols, couple_vals):
    inv_root = 1.0 / math.sqrt(M)
    block_starts = jnp.arange(M // row_block, dtype=jnp.int32) * row_block
    outputs = []
    for slab_index in range(SLABS):
        green_slab = green_blocks[:, slab_index]
        coulomb_block = coulomb[slab_index]

        def polar_rows(start):
            rows_now = lax.dynamic_slice_in_dim(green_slab, start, row_block, 1).astype(jnp.float32)
            mirror = jnp.swapaxes(lax.dynamic_slice_in_dim(green_slab, start, row_block, 2), 1, 2).astype(jnp.float32)
            spectra = jnp.fft.fft(rows_now, axis=0) * jnp.conj(jnp.fft.fft(mirror, axis=0))
            return jnp.real(jnp.fft.ifft(spectra, axis=0)).astype(jnp.float32)
        polar = jnp.swapaxes(lax.map(polar_rows, block_starts), 0, 1).reshape(NE, M, M)
        polar = (polar * (0.5 / math.sqrt(M * NE))).astype(jnp.bfloat16)
        screened = lax.map(lambda polar_one: screen(polar_one, coulomb_block), polar)
        screened = lax.optimization_barrier(screened)

        def sigma_rows(start):
            rows_now = lax.dynamic_slice_in_dim(green_slab, start, row_block, 1).astype(jnp.float32)
            waves = lax.dynamic_slice_in_dim(screened, start, row_block, 1).astype(jnp.float32)
            spectra = jnp.fft.fft(rows_now, axis=0) * jnp.fft.fft(waves, axis=0)
            return jnp.real(jnp.fft.ifft(spectra, axis=0)).astype(jnp.float32)
        sigma = jnp.swapaxes(lax.map(sigma_rows, block_starts), 0, 1).reshape(NE, M, M)
        sigma = (sigma * (0.2 / math.sqrt(NE))).astype(jnp.bfloat16)
        total = sigma.astype(jnp.float32)
        last = M - IFACE
        if slab_index + 1 < SLABS:
            coupling = coupling_matrix(couple_cols[slab_index], couple_vals[slab_index])
            corner = green_blocks[:, slab_index + 1, :IFACE, :IFACE]
            near_next = jnp.einsum('ij,ejk->eik', coupling.astype(jnp.float32), corner.astype(jnp.float32))
            near_next = lax.optimization_barrier(near_next.astype(jnp.bfloat16))
            right_part = jnp.einsum('eij,kj->eik', near_next.astype(jnp.float32), coupling.astype(jnp.float32)) * inv_root
            total = total.at[:, last:, last:].add(right_part)
        if slab_index > 0:
            previous = coupling_matrix(couple_cols[slab_index - 1], couple_vals[slab_index - 1])
            corner = green_blocks[:, slab_index - 1, last:, last:]
            near_prev = jnp.einsum('ji,ejk->eik', previous.astype(jnp.float32), corner.astype(jnp.float32))
            near_prev = lax.optimization_barrier(near_prev.astype(jnp.bfloat16))
            left_part = jnp.einsum('eij,jk->eik', near_prev.astype(jnp.float32), previous.astype(jnp.float32)) * inv_root
            total = total.at[:, :IFACE, :IFACE].add(left_part)
        total_b = lax.optimization_barrier(total.astype(jnp.bfloat16))
        dressed = lax.optimization_barrier(batched(green_slab, total_b).astype(jnp.bfloat16))
        updated = green_slab.astype(jnp.float32) + batched(dressed, green_slab) * inv_root
        outputs.append(updated.astype(jnp.bfloat16))
    return jnp.stack(outputs, axis=1)
```

```python
import functools
import math

import jax
import jax.numpy as jnp
import ml_dtypes
import numpy as np
from jax import lax
from jax.experimental import pallas as pl
from jax.experimental.pallas import tpu as pltpu
from jax.sharding import PartitionSpec as P

BLOCK = 128
ROWS = 8
OWNERS = BLOCK // ROWS
LIMIT = 40 * 1024 * 1024


def pairs_of(blocks):
    apart = [(a, b) for a in range(blocks) for b in range(a + 1, blocks)]
    return apart, [(a, a + 1) for a in range(0, blocks, 2)]


def dot(left, right):
    return jnp.dot(left, right, preferred_element_type=jnp.float32)


def parts(values):
    high = values.astype(jnp.bfloat16)
    return high, (values - high.astype(jnp.float32)).astype(jnp.bfloat16)


def triangle():
    row = lax.broadcasted_iota(jnp.int32, (BLOCK, BLOCK), 0)
    column = lax.broadcasted_iota(jnp.int32, (BLOCK, BLOCK), 1)
    return row <= column, row < column


def pack(block, blocks, out_ref):
    apart, diagonal = pairs_of(blocks)
    upper, above = triangle()
    for p, (a, b) in enumerate(apart + diagonal):
        if p < len(apart):
            first, second = block(a, b), block(b, a).T
        else:
            one, two = block(a, a), block(b, b)
            first, second = jnp.where(upper, one, two), jnp.where(above, one.T, two.T)
        both = jnp.concatenate(
            [first.reshape(OWNERS, ROWS, BLOCK), second.reshape(OWNERS, ROWS, BLOCK)], axis=1
        )
        out_ref[p * OWNERS : (p + 1) * OWNERS] = both.astype(jnp.bfloat16)


def unpack(in_ref, blocks, store):
    apart, diagonal = pairs_of(blocks)
    upper, _ = triangle()
    for p, (a, b) in enumerate(apart + diagonal):
        both = in_ref[p * OWNERS : (p + 1) * OWNERS].astype(jnp.float32)
        first = both[:, :ROWS].reshape(BLOCK, BLOCK)
        second = both[:, ROWS:].reshape(BLOCK, BLOCK).T
        if p < len(apart):
            store(a, b, first)
            store(b, a, second)
        else:
            store(a, a, jnp.where(upper, first, second))
            store(b, b, jnp.where(upper, second, first))


def at(a, b):
    return pl.ds(a * BLOCK, BLOCK), pl.ds(b * BLOCK, BLOCK)


def pack_kernel(blocks, green_ref, out_ref):
    pack(lambda a, b: green_ref[at(a, b)].astype(jnp.float32), blocks, out_ref)


def forward(table_ref, entries):
    return dot(table_ref[...], jnp.concatenate([entries, entries], axis=0))


def backward(table_ref, real, imag):
    high, low = parts(jnp.concatenate([real, imag], axis=0))
    return dot(table_ref[...], jnp.concatenate([high, low, high], axis=0))


def polar_kernel(entries_ref, own_ref, forward_ref, backward_ref, spectrum_ref, out_ref):
    spectrum = forward(forward_ref, entries_ref[...])
    spectrum_ref[...] = spectrum
    half, width = spectrum.shape[0] // 2, spectrum.shape[1] // 2
    edge = lax.broadcasted_iota(jnp.int32, (half, width), 0) == 0
    own = own_ref[...] > 0.5
    real = spectrum[:half, :width], spectrum[:half, width:]
    imag = spectrum[half:, :width], spectrum[half:, width:]
    for slot in range(2):
        mirror_real = jnp.where(own, real[slot], real[1 - slot])
        mirror_imag = jnp.where(own, imag[slot], imag[1 - slot])
        rr, ii = real[slot] * mirror_real, imag[slot] * mirror_imag
        ir, ri = imag[slot] * mirror_real, real[slot] * mirror_imag
        values = backward(backward_ref, jnp.where(edge, rr, rr + ii), jnp.where(edge, ii, ir - ri))
        out_ref[:, slot * width : (slot + 1) * width] = values.astype(jnp.bfloat16)


def screen_kernel(blocks, polar_ref, coulomb_ref, out_ref, matrix_ref, screened_ref):
    def store(a, b, value):
        matrix_ref[at(a, b)] = value.astype(jnp.bfloat16)

    unpack(polar_ref, blocks, store)
    coulomb = coulomb_ref[...]
    inner = dot(coulomb, matrix_ref[...]).astype(jnp.bfloat16)
    second = dot(inner, coulomb)
    third = dot(inner, second.astype(jnp.bfloat16))
    screened = (coulomb.astype(jnp.float32) + second + third).astype(jnp.bfloat16)
    screened_ref[...] = screened.astype(jnp.float32)
    pack(lambda a, b: screened_ref[at(a, b)], blocks, out_ref)


def sigma_kernel(entries_ref, green_ref, forward_ref, backward_ref, out_ref):
    spectrum = forward(forward_ref, entries_ref[...])
    half = spectrum.shape[0] // 2
    edge = lax.broadcasted_iota(jnp.int32, (half, spectrum.shape[1]), 0) == 0
    real, imag = spectrum[:half], spectrum[half:]
    green_real, green_imag = green_ref[:half], green_ref[half:]
    rr, ii = green_real * real, green_imag * imag
    cross = green_real * imag + green_imag * real
    values = backward(backward_ref, jnp.where(edge, rr, rr - ii), jnp.where(edge, ii, cross))
    out_ref[...] = values.astype(jnp.bfloat16)


def final_kernel(blocks, inv_root, sigma_ref, green_ref, right_ref, left_ref, out_ref, total_ref):
    def store(a, b, value):
        if a == b == blocks - 1:
            value = value + right_ref[...]
        if a == b == 0:
            value = value + left_ref[...]
        total_ref[at(a, b)] = value.astype(jnp.bfloat16)

    unpack(sigma_ref, blocks, store)
    green = green_ref[...]
    dressed = dot(green, total_ref[...]).astype(jnp.bfloat16)
    updated = green.astype(jnp.float32) + dot(dressed, green) * inv_root
    out_ref[...] = updated.astype(jnp.bfloat16)


def call(kernel, outs, scratch=(), flops=0, moved=0):
    return pl.pallas_call(
        kernel,
        out_shape=outs,
        scratch_shapes=list(scratch),
        compiler_params=pltpu.CompilerParams(vmem_limit_bytes=LIMIT),
        cost_estimate=pl.CostEstimate(flops=flops, bytes_accessed=moved, transcendentals=0),
    )


def tables(energies, scale):
    half = energies // 2
    turns = np.outer(np.arange(half), np.arange(energies)) % energies
    angle = turns * (2.0 * math.pi / energies)
    cosine, sine = np.cos(angle), -np.sin(angle)
    sine[0] = np.cos(math.pi * np.arange(energies))
    weights = np.full((half, 1), 2.0 / energies)
    weights[0] = 1.0 / energies
    ahead = np.concatenate([cosine, sine], axis=0)
    back = np.concatenate([cosine * weights, sine * weights], axis=0).T

    def two(table):
        high = table.astype(ml_dtypes.bfloat16)
        return high, (table - high.astype(np.float64)).astype(ml_dtypes.bfloat16)

    ahead_high, ahead_low = two(ahead)
    result = [np.concatenate([ahead_high, ahead_low], axis=1)]
    for factor in scale:
        high, low = two(back * factor)
        result.append(np.concatenate([high, high, low], axis=1))
    return [jnp.asarray(t) for t in result]


def coupling_matrix(column_ids, coupling_values):
    width = column_ids.shape[0]
    hits = column_ids[:, :, None] == jnp.arange(width, dtype=jnp.int32)[None, None, :]
    summed = jnp.sum(
        jnp.where(hits, coupling_values.astype(jnp.float32)[:, :, None], jnp.float32(0.0)), axis=1
    )
    return summed.astype(jnp.bfloat16)


def from_behind(x, axis, by):
    size = lax.axis_size(axis)
    pairs = [(i, i + by) for i in range(size) if 0 <= i + by < size]
    return lax.ppermute(x, axis, pairs)


def exchange(x):
    return lax.all_to_all(x, "energy", split_axis=0, concat_axis=0, tiled=True)


def on_device(green_blocks, coulomb, couple_cols, couple_vals):
    green, coulomb_block = green_blocks[0, 0], coulomb[0]
    orbitals = green.shape[0]
    blocks = orbitals // BLOCK
    energies = lax.axis_size("energy")
    chunk = (energies, 2 * ROWS, BLOCK)
    flat = (energies, 2 * ROWS * BLOCK)
    f32, b16 = jnp.float32, jnp.bfloat16
    ahead, back_polar, back_sigma = tables(
        energies, (0.5 / math.sqrt(orbitals * energies), 0.2 / math.sqrt(energies))
    )

    packed = call(functools.partial(pack_kernel, blocks), jax.ShapeDtypeStruct(chunk, b16))(green)
    entries = exchange(packed).reshape(flat)

    owner = lax.axis_index("energy")
    column = jnp.arange(ROWS * BLOCK, dtype=jnp.int32)
    row = lax.rem(owner, OWNERS) * ROWS + column // BLOCK
    shares = owner >= energies - (blocks // 2) * OWNERS
    own = ((row == column % BLOCK) & shares).astype(f32)[None]

    spectrum, polar = call(
        polar_kernel, (jax.ShapeDtypeStruct(flat, f32), jax.ShapeDtypeStruct(flat, b16))
    )(entries, own, ahead, back_polar)
    polar = exchange(polar.reshape(chunk))

    screened = call(
        functools.partial(screen_kernel, blocks),
        jax.ShapeDtypeStruct(chunk, b16),
        (pltpu.VMEM((orbitals, orbitals), b16), pltpu.VMEM((orbitals, orbitals), f32)),
    )(polar, coulomb_block)
    screened = exchange(screened).reshape(flat)

    sigma = call(sigma_kernel, jax.ShapeDtypeStruct(flat, b16))(
        screened, spectrum, ahead, back_sigma
    )
    sigma = exchange(sigma.reshape(chunk))

    interface = couple_cols.shape[1]
    last = orbitals - interface
    inv_root = 1.0 / math.sqrt(orbitals)
    coupling = coupling_matrix(couple_cols[0], couple_vals[0])
    behind = from_behind(jnp.concatenate([green[last:, last:], coupling], axis=0), "slab", 1)
    prev_corner, previous = behind[:interface], behind[interface:]
    next_corner = from_behind(green[:interface, :interface], "slab", -1)
    near_next = dot(coupling, next_corner).astype(b16)
    near_prev = dot(previous.T, prev_corner).astype(b16)
    right_part = dot(near_next, coupling.T) * inv_root
    left_part = dot(near_prev, previous) * inv_root

    updated = call(
        functools.partial(final_kernel, blocks, inv_root),
        jax.ShapeDtypeStruct((orbitals, orbitals), b16),
        (pltpu.VMEM((orbitals, orbitals), b16),),
    )(sigma, green, right_part, left_part)
    return updated[None, None]


def solution(mesh):
    return jax.shard_map(
        on_device,
        mesh=mesh,
        in_specs=(
            P("energy", "slab", None, None),
            P("slab", None, None),
            P("slab", None, None),
            P("slab", None, None),
        ),
        out_specs=P("energy", "slab", None, None),
        check_vma=False,
    )
```

```python
import functools
import math

import jax
import jax.numpy as jnp
from jax import lax
from jax.experimental import pallas as pl
from jax.experimental.pallas import tpu as pltpu
from jax.sharding import PartitionSpec as P

BLOCK = 128
ROWS = 8
OWNERS = BLOCK // ROWS
LIMIT = 40 * 1024 * 1024


def pairs_of(blocks):
    apart = [(a, b) for a in range(blocks) for b in range(a + 1, blocks)]
    return apart, [(a, a + 1) for a in range(0, blocks, 2)]


def dot(left, right):
    return jnp.dot(left, right, preferred_element_type=jnp.float32)


def parts(values):
    high = values.astype(jnp.bfloat16)
    return high, (values - high.astype(jnp.float32)).astype(jnp.bfloat16)


def triangle():
    row = lax.broadcasted_iota(jnp.int32, (BLOCK, BLOCK), 0)
    column = lax.broadcasted_iota(jnp.int32, (BLOCK, BLOCK), 1)
    return row <= column, row < column


def pack(block, blocks, out_ref):
    apart, diagonal = pairs_of(blocks)
    upper, above = triangle()
    for p, (a, b) in enumerate(apart + diagonal):
        if p < len(apart):
            first, second = block(a, b), block(b, a).T
        else:
            one, two = block(a, a), block(b, b)
            first, second = jnp.where(upper, one, two), jnp.where(above, one.T, two.T)
        both = jnp.concatenate(
            [first.reshape(OWNERS, ROWS, BLOCK), second.reshape(OWNERS, ROWS, BLOCK)], axis=1
        )
        out_ref[p * OWNERS : (p + 1) * OWNERS] = both.astype(jnp.bfloat16)


def unpack(in_ref, blocks, store):
    apart, diagonal = pairs_of(blocks)
    upper, _ = triangle()
    for p, (a, b) in enumerate(apart + diagonal):
        both = in_ref[p * OWNERS : (p + 1) * OWNERS].astype(jnp.float32)
        first = both[:, :ROWS].reshape(BLOCK, BLOCK)
        second = both[:, ROWS:].reshape(BLOCK, BLOCK).T
        if p < len(apart):
            store(a, b, first)
            store(b, a, second)
        else:
            store(a, a, jnp.where(upper, first, second))
            store(b, b, jnp.where(upper, second, first))


def at(a, b):
    return pl.ds(a * BLOCK, BLOCK), pl.ds(b * BLOCK, BLOCK)


def pack_kernel(blocks, green_ref, out_ref):
    pack(lambda a, b: green_ref[at(a, b)].astype(jnp.float32), blocks, out_ref)


def forward(table_ref, entries):
    return dot(table_ref[...], jnp.concatenate([entries, entries], axis=0))


def backward(table_ref, real, imag):
    high, low = parts(jnp.concatenate([real, imag], axis=0))
    return dot(table_ref[...], jnp.concatenate([high, low, high], axis=0))


def polar_kernel(scale, entries_ref, own_ref, forward_ref, backward_ref, spectrum_ref, out_ref):
    spectrum = forward(forward_ref, entries_ref[...])
    spectrum_ref[...] = spectrum
    half, width = spectrum.shape[0] // 2, spectrum.shape[1] // 2
    edge = lax.broadcasted_iota(jnp.int32, (half, width), 0) == 0
    own = own_ref[...] > 0.5
    real = spectrum[:half, :width], spectrum[:half, width:]
    imag = spectrum[half:, :width], spectrum[half:, width:]
    for slot in range(2):
        mirror_real = jnp.where(own, real[slot], real[1 - slot])
        mirror_imag = jnp.where(own, imag[slot], imag[1 - slot])
        rr, ii = real[slot] * mirror_real, imag[slot] * mirror_imag
        ir, ri = imag[slot] * mirror_real, real[slot] * mirror_imag
        values = backward(backward_ref, jnp.where(edge, rr, rr + ii), jnp.where(edge, ii, ir - ri))
        out_ref[:, slot * width : (slot + 1) * width] = (values * scale).astype(jnp.bfloat16)


def screen_kernel(blocks, polar_ref, coulomb_ref, out_ref, matrix_ref, screened_ref):
    def store(a, b, value):
        matrix_ref[at(a, b)] = value.astype(jnp.bfloat16)

    unpack(polar_ref, blocks, store)
    coulomb = coulomb_ref[...]
    inner = dot(coulomb, matrix_ref[...]).astype(jnp.bfloat16)
    second = dot(inner, coulomb)
    third = dot(inner, second.astype(jnp.bfloat16))
    screened = (coulomb.astype(jnp.float32) + second + third).astype(jnp.bfloat16)
    screened_ref[...] = screened.astype(jnp.float32)
    pack(lambda a, b: screened_ref[at(a, b)], blocks, out_ref)


def sigma_kernel(scale, entries_ref, green_ref, forward_ref, backward_ref, out_ref):
    spectrum = forward(forward_ref, entries_ref[...])
    half = spectrum.shape[0] // 2
    edge = lax.broadcasted_iota(jnp.int32, (half, spectrum.shape[1]), 0) == 0
    real, imag = spectrum[:half], spectrum[half:]
    green_real, green_imag = green_ref[:half], green_ref[half:]
    rr, ii = green_real * real, green_imag * imag
    cross = green_real * imag + green_imag * real
    values = backward(backward_ref, jnp.where(edge, rr, rr - ii), jnp.where(edge, ii, cross))
    out_ref[...] = (values * scale).astype(jnp.bfloat16)


def final_kernel(blocks, inv_root, sigma_ref, green_ref, right_ref, left_ref, out_ref, total_ref):
    def store(a, b, value):
        if a == b == blocks - 1:
            value = value + right_ref[...]
        if a == b == 0:
            value = value + left_ref[...]
        total_ref[at(a, b)] = value.astype(jnp.bfloat16)

    unpack(sigma_ref, blocks, store)
    green = green_ref[...]
    dressed = dot(green, total_ref[...]).astype(jnp.bfloat16)
    updated = green.astype(jnp.float32) + dot(dressed, green) * inv_root
    out_ref[...] = updated.astype(jnp.bfloat16)


def call(kernel, outs, scratch=(), flops=0, moved=0):
    return pl.pallas_call(
        kernel,
        out_shape=outs,
        scratch_shapes=list(scratch),
        compiler_params=pltpu.CompilerParams(vmem_limit_bytes=LIMIT),
        cost_estimate=pl.CostEstimate(flops=flops, bytes_accessed=moved, transcendentals=0),
    )


def tables(energies):
    half = energies // 2
    frequency = jnp.arange(half, dtype=jnp.int32)
    energy = jnp.arange(energies, dtype=jnp.int32)
    turns = (frequency[:, None] * energy[None, :]) % energies
    angle = turns.astype(jnp.float32) * (2.0 * math.pi / energies)
    first = frequency[:, None] == 0
    cosine = jnp.cos(angle)
    sine = jnp.where(first, (1 - 2 * (energy % 2)).astype(jnp.float32)[None], -jnp.sin(angle))
    weights = jnp.where(first, 1.0, 2.0).astype(jnp.float32) / energies
    ahead_high, ahead_low = parts(jnp.concatenate([cosine, sine], axis=0))
    back_high, back_low = parts(jnp.concatenate([cosine * weights, sine * weights], axis=0).T)
    return (
        jnp.concatenate([ahead_high, ahead_low], axis=1),
        jnp.concatenate([back_high, back_high, back_low], axis=1),
    )


def coupling_matrix(column_ids, coupling_values):
    width = column_ids.shape[0]
    hits = column_ids[:, :, None] == jnp.arange(width, dtype=jnp.int32)[None, None, :]
    summed = jnp.sum(
        jnp.where(hits, coupling_values.astype(jnp.float32)[:, :, None], jnp.float32(0.0)), axis=1
    )
    return summed.astype(jnp.bfloat16)


def from_behind(x, axis, by):
    size = lax.axis_size(axis)
    pairs = [(i, i + by) for i in range(size) if 0 <= i + by < size]
    return lax.ppermute(x, axis, pairs)


def exchange(x):
    return lax.all_to_all(x, "energy", split_axis=0, concat_axis=0, tiled=True)


def on_device(green_blocks, coulomb, couple_cols, couple_vals):
    green, coulomb_block = green_blocks[0, 0], coulomb[0]
    orbitals = green.shape[0]
    blocks = orbitals // BLOCK
    energies = lax.axis_size("energy")
    chunk = (energies, 2 * ROWS, BLOCK)
    flat = (energies, 2 * ROWS * BLOCK)
    f32, b16 = jnp.float32, jnp.bfloat16
    packed = call(functools.partial(pack_kernel, blocks), jax.ShapeDtypeStruct(chunk, b16))(green)
    packed, corners = lax.optimization_barrier((packed, green))
    entries = exchange(packed)

    ahead, back = tables(energies)
    owner = lax.axis_index("energy")
    column = jnp.arange(ROWS * BLOCK, dtype=jnp.int32)
    row = lax.rem(owner, OWNERS) * ROWS + column // BLOCK
    shares = owner >= energies - (blocks // 2) * OWNERS
    own = ((row == column % BLOCK) & shares).astype(f32)[None]

    interface = couple_cols.shape[1]
    last = orbitals - interface
    inv_root = 1.0 / math.sqrt(orbitals)
    coupling = coupling_matrix(couple_cols[0], couple_vals[0])
    behind = from_behind(jnp.concatenate([corners[last:, last:], coupling], axis=0), "slab", 1)
    prev_corner, previous = behind[:interface], behind[interface:]
    next_corner = from_behind(corners[:interface, :interface], "slab", -1)
    near_next = dot(coupling, next_corner).astype(b16)
    near_prev = dot(previous.T, prev_corner).astype(b16)
    right_part = dot(near_next, coupling.T) * inv_root
    left_part = dot(near_prev, previous) * inv_root
    entries, ahead, back, own, right_part, left_part = lax.optimization_barrier(
        (entries, ahead, back, own, right_part, left_part)
    )

    spectrum, polar = call(
        functools.partial(polar_kernel, 0.5 / math.sqrt(orbitals * energies)),
        (jax.ShapeDtypeStruct(flat, f32), jax.ShapeDtypeStruct(flat, b16)),
    )(entries.reshape(flat), own, ahead, back)
    polar = exchange(polar.reshape(chunk))

    screened = call(
        functools.partial(screen_kernel, blocks),
        jax.ShapeDtypeStruct(chunk, b16),
        (pltpu.VMEM((orbitals, orbitals), b16), pltpu.VMEM((orbitals, orbitals), f32)),
    )(polar, coulomb_block)
    screened = exchange(screened).reshape(flat)

    sigma = call(
        functools.partial(sigma_kernel, 0.2 / math.sqrt(energies)),
        jax.ShapeDtypeStruct(flat, b16),
    )(screened, spectrum, ahead, back)
    sigma = exchange(sigma.reshape(chunk))

    updated = call(
        functools.partial(final_kernel, blocks, inv_root),
        jax.ShapeDtypeStruct((orbitals, orbitals), b16),
        (pltpu.VMEM((orbitals, orbitals), b16),),
    )(sigma, green, right_part, left_part)
    return updated[None, None]


def solution(mesh):
    return jax.shard_map(
        on_device,
        mesh=mesh,
        in_specs=(
            P("energy", "slab", None, None),
            P("slab", None, None),
            P("slab", None, None),
            P("slab", None, None),
        ),
        out_specs=P("energy", "slab", None, None),
        check_vma=False,
    )
```

```python
import functools
import math

import jax
import jax.numpy as jnp
from jax import lax
from jax.experimental import pallas as pl
from jax.experimental.pallas import tpu as pltpu
from jax.sharding import PartitionSpec as P

BLOCK = 128
ROWS = 8
OWNERS = BLOCK // ROWS
LIMIT = 40 * 1024 * 1024


def pairs_of(blocks):
    apart = [(a, b) for a in range(blocks) for b in range(a + 1, blocks)]
    return apart, [(a, a + 1) for a in range(0, blocks, 2)]


def dot(left, right):
    return jnp.dot(left, right, preferred_element_type=jnp.float32)


def parts(values):
    high = values.astype(jnp.bfloat16)
    return high, (values - high.astype(jnp.float32)).astype(jnp.bfloat16)


def triangle():
    row = lax.broadcasted_iota(jnp.int32, (BLOCK, BLOCK), 0)
    column = lax.broadcasted_iota(jnp.int32, (BLOCK, BLOCK), 1)
    return row <= column, row < column


def pack(block, blocks, out_ref):
    apart, diagonal = pairs_of(blocks)
    upper, above = triangle()
    for p, (a, b) in enumerate(apart + diagonal):
        if p < len(apart):
            first, second = block(a, b), block(b, a).T
        else:
            one, two = block(a, a), block(b, b)
            first, second = jnp.where(upper, one, two), jnp.where(above, one.T, two.T)
        both = jnp.concatenate(
            [first.reshape(OWNERS, ROWS, BLOCK), second.reshape(OWNERS, ROWS, BLOCK)], axis=1
        )
        out_ref[p * OWNERS : (p + 1) * OWNERS] = both.astype(jnp.bfloat16)


def unpack(in_ref, blocks, store):
    apart, diagonal = pairs_of(blocks)
    upper, _ = triangle()
    for p, (a, b) in enumerate(apart + diagonal):
        both = in_ref[p * OWNERS : (p + 1) * OWNERS].astype(jnp.float32)
        first = both[:, :ROWS].reshape(BLOCK, BLOCK)
        second = both[:, ROWS:].reshape(BLOCK, BLOCK).T
        if p < len(apart):
            store(a, b, first)
            store(b, a, second)
        else:
            store(a, a, jnp.where(upper, first, second))
            store(b, b, jnp.where(upper, second, first))


def at(a, b):
    return pl.ds(a * BLOCK, BLOCK), pl.ds(b * BLOCK, BLOCK)


def pack_kernel(blocks, green_ref, out_ref):
    pack(lambda a, b: green_ref[at(a, b)].astype(jnp.float32), blocks, out_ref)


def forward(table_ref, entries):
    return dot(table_ref[...], entries)


def backward(table_ref, real, imag):
    high, low = parts(jnp.concatenate([real, imag], axis=0))
    return dot(table_ref[...], jnp.concatenate([high, low], axis=0))


def polar_kernel(scale, entries_ref, own_ref, forward_ref, backward_ref, spectrum_ref, out_ref):
    spectrum = forward(forward_ref, entries_ref[...])
    spectrum_ref[...] = spectrum
    half, width = spectrum.shape[0] // 2, spectrum.shape[1] // 2
    edge = lax.broadcasted_iota(jnp.int32, (half, width), 0) == 0
    own = own_ref[...] > 0.5
    real = spectrum[:half, :width], spectrum[:half, width:]
    imag = spectrum[half:, :width], spectrum[half:, width:]
    for slot in range(2):
        mirror_real = jnp.where(own, real[slot], real[1 - slot])
        mirror_imag = jnp.where(own, imag[slot], imag[1 - slot])
        rr, ii = real[slot] * mirror_real, imag[slot] * mirror_imag
        ir, ri = imag[slot] * mirror_real, real[slot] * mirror_imag
        values = backward(backward_ref, jnp.where(edge, rr, rr + ii), jnp.where(edge, ii, ir - ri))
        out_ref[:, slot * width : (slot + 1) * width] = (values * scale).astype(jnp.bfloat16)


def screen_kernel(blocks, polar_ref, coulomb_ref, out_ref, matrix_ref, screened_ref):
    def store(a, b, value):
        matrix_ref[at(a, b)] = value.astype(jnp.bfloat16)

    unpack(polar_ref, blocks, store)
    coulomb = coulomb_ref[...]
    inner = dot(coulomb, matrix_ref[...]).astype(jnp.bfloat16)
    second = dot(inner, coulomb)
    third = dot(inner, second.astype(jnp.bfloat16))
    screened = (coulomb.astype(jnp.float32) + second + third).astype(jnp.bfloat16)
    screened_ref[...] = screened.astype(jnp.float32)
    pack(lambda a, b: screened_ref[at(a, b)], blocks, out_ref)


def sigma_kernel(scale, entries_ref, green_ref, forward_ref, backward_ref, out_ref):
    spectrum = forward(forward_ref, entries_ref[...])
    half = spectrum.shape[0] // 2
    edge = lax.broadcasted_iota(jnp.int32, (half, spectrum.shape[1]), 0) == 0
    real, imag = spectrum[:half], spectrum[half:]
    green_real, green_imag = green_ref[:half], green_ref[half:]
    rr, ii = green_real * real, green_imag * imag
    cross = green_real * imag + green_imag * real
    values = backward(backward_ref, jnp.where(edge, rr, rr - ii), jnp.where(edge, ii, cross))
    out_ref[...] = (values * scale).astype(jnp.bfloat16)


def final_kernel(blocks, inv_root, sigma_ref, green_ref, right_ref, left_ref, out_ref, total_ref):
    def store(a, b, value):
        if a == b == blocks - 1:
            value = value + right_ref[...]
        if a == b == 0:
            value = value + left_ref[...]
        total_ref[at(a, b)] = value.astype(jnp.bfloat16)

    unpack(sigma_ref, blocks, store)
    green = green_ref[...]
    dressed = dot(green, total_ref[...]).astype(jnp.bfloat16)
    updated = green.astype(jnp.float32) + dot(dressed, green) * inv_root
    out_ref[...] = updated.astype(jnp.bfloat16)


def call(kernel, outs, scratch=(), flops=0, moved=0):
    return pl.pallas_call(
        kernel,
        out_shape=outs,
        scratch_shapes=list(scratch),
        compiler_params=pltpu.CompilerParams(vmem_limit_bytes=LIMIT),
        cost_estimate=pl.CostEstimate(flops=flops, bytes_accessed=moved, transcendentals=0),
    )


def tables(energies):
    half = energies // 2

    def waves(shape, along):
        row = lax.broadcasted_iota(jnp.int32, shape, along)
        energy = lax.broadcasted_iota(jnp.int32, shape, 1 - along)
        frequency = row % half
        angle = ((frequency * energy) % energies).astype(jnp.float32) * (2.0 * math.pi / energies)
        nyquist = (1 - 2 * (energy % 2)).astype(jnp.float32)
        sine = jnp.where(frequency == 0, nyquist, -jnp.sin(angle))
        return jnp.where(row < half, jnp.cos(angle), sine), frequency == 0

    square = (energies, energies)
    ahead, _ = waves(square, 0)
    back, first = waves(square, 1)
    back = (back * (jnp.where(first, 1.0, 2.0) / energies)).astype(jnp.bfloat16)
    return ahead.astype(jnp.bfloat16), jnp.concatenate([back, back], axis=1)


def coupling_matrix(column_ids, coupling_values):
    width = column_ids.shape[0]
    hits = column_ids[:, :, None] == jnp.arange(width, dtype=jnp.int32)[None, None, :]
    summed = jnp.sum(
        jnp.where(hits, coupling_values.astype(jnp.float32)[:, :, None], jnp.float32(0.0)), axis=1
    )
    return summed.astype(jnp.bfloat16)


def from_behind(x, axis, by):
    size = lax.axis_size(axis)
    pairs = [(i, i + by) for i in range(size) if 0 <= i + by < size]
    return lax.ppermute(x, axis, pairs)


def exchange(x):
    return lax.all_to_all(x, "energy", split_axis=0, concat_axis=0, tiled=True)


def on_device(green_blocks, coulomb, couple_cols, couple_vals):
    green, coulomb_block = green_blocks[0, 0], coulomb[0]
    orbitals = green.shape[0]
    blocks = orbitals // BLOCK
    energies = lax.axis_size("energy")
    chunk = (energies, 2 * ROWS, BLOCK)
    flat = (energies, 2 * ROWS * BLOCK)
    f32, b16 = jnp.float32, jnp.bfloat16
    packed = call(functools.partial(pack_kernel, blocks), jax.ShapeDtypeStruct(chunk, b16))(green)
    packed, corners = lax.optimization_barrier((packed, green))
    entries = exchange(packed)

    ahead, back = tables(energies)
    owner = lax.axis_index("energy")
    column = jnp.arange(ROWS * BLOCK, dtype=jnp.int32)
    row = lax.rem(owner, OWNERS) * ROWS + column // BLOCK
    shares = owner >= energies - (blocks // 2) * OWNERS
    own = ((row == column % BLOCK) & shares).astype(f32)[None]

    interface = couple_cols.shape[1]
    last = orbitals - interface
    inv_root = 1.0 / math.sqrt(orbitals)
    coupling = coupling_matrix(couple_cols[0], couple_vals[0])
    behind = from_behind(jnp.concatenate([corners[last:, last:], coupling], axis=0), "slab", 1)
    prev_corner, previous = behind[:interface], behind[interface:]
    next_corner = from_behind(corners[:interface, :interface], "slab", -1)
    near_next = dot(coupling, next_corner).astype(b16)
    near_prev = dot(previous.T, prev_corner).astype(b16)
    right_part = dot(near_next, coupling.T) * inv_root
    left_part = dot(near_prev, previous) * inv_root
    entries, ahead, back, own, right_part, left_part = lax.optimization_barrier(
        (entries, ahead, back, own, right_part, left_part)
    )

    spectrum, polar = call(
        functools.partial(polar_kernel, 0.5 / math.sqrt(orbitals * energies)),
        (jax.ShapeDtypeStruct(flat, f32), jax.ShapeDtypeStruct(flat, b16)),
    )(entries.reshape(flat), own, ahead, back)
    polar = exchange(polar.reshape(chunk))

    screened = call(
        functools.partial(screen_kernel, blocks),
        jax.ShapeDtypeStruct(chunk, b16),
        (pltpu.VMEM((orbitals, orbitals), b16), pltpu.VMEM((orbitals, orbitals), f32)),
    )(polar, coulomb_block)
    screened = exchange(screened).reshape(flat)

    sigma = call(
        functools.partial(sigma_kernel, 0.2 / math.sqrt(energies)),
        jax.ShapeDtypeStruct(flat, b16),
    )(screened, spectrum, ahead, back)
    sigma = exchange(sigma.reshape(chunk))

    updated = call(
        functools.partial(final_kernel, blocks, inv_root),
        jax.ShapeDtypeStruct((orbitals, orbitals), b16),
        (pltpu.VMEM((orbitals, orbitals), b16),),
    )(sigma, green, right_part, left_part)
    return updated[None, None]


def solution(mesh):
    return jax.shard_map(
        on_device,
        mesh=mesh,
        in_specs=(
            P("energy", "slab", None, None),
            P("slab", None, None),
            P("slab", None, None),
            P("slab", None, None),
        ),
        out_specs=P("energy", "slab", None, None),
        check_vma=False,
    )
```

```python
import functools
import math

import jax
import jax.numpy as jnp
from jax import lax
from jax.experimental import pallas as pl
from jax.experimental.pallas import tpu as pltpu
from jax.sharding import PartitionSpec as P

BLOCK = 128
ROWS = 8
OWNERS = BLOCK // ROWS
LIMIT = 40 * 1024 * 1024


def pairs_of(blocks):
    apart = [(a, b) for a in range(blocks) for b in range(a + 1, blocks)]
    return apart, [(a, a + 1) for a in range(0, blocks, 2)]


def dot(left, right):
    return jnp.dot(left, right, preferred_element_type=jnp.float32)


def parts(values):
    high = values.astype(jnp.bfloat16)
    return high, (values - high.astype(jnp.float32)).astype(jnp.bfloat16)


def triangle():
    row = lax.broadcasted_iota(jnp.int32, (BLOCK, BLOCK), 0)
    column = lax.broadcasted_iota(jnp.int32, (BLOCK, BLOCK), 1)
    return row <= column, row < column


def pack(block, blocks, out_ref):
    apart, diagonal = pairs_of(blocks)
    upper, above = triangle()
    for p, (a, b) in enumerate(apart + diagonal):
        if p < len(apart):
            first, second = block(a, b), block(b, a).T
        else:
            one, two = block(a, a), block(b, b)
            first, second = jnp.where(upper, one, two), jnp.where(above, one.T, two.T)
        both = jnp.concatenate(
            [first.reshape(OWNERS, ROWS, BLOCK), second.reshape(OWNERS, ROWS, BLOCK)], axis=1
        )
        out_ref[p * OWNERS : (p + 1) * OWNERS] = both.astype(jnp.bfloat16)


def unpack(in_ref, blocks, store):
    apart, diagonal = pairs_of(blocks)
    upper, _ = triangle()
    for p, (a, b) in enumerate(apart + diagonal):
        both = in_ref[p * OWNERS : (p + 1) * OWNERS].astype(jnp.float32)
        first = both[:, :ROWS].reshape(BLOCK, BLOCK)
        second = both[:, ROWS:].reshape(BLOCK, BLOCK).T
        if p < len(apart):
            store(a, b, first)
            store(b, a, second)
        else:
            store(a, a, jnp.where(upper, first, second))
            store(b, b, jnp.where(upper, second, first))


def at(a, b):
    return pl.ds(a * BLOCK, BLOCK), pl.ds(b * BLOCK, BLOCK)


def pack_kernel(blocks, green_ref, out_ref):
    pack(lambda a, b: green_ref[at(a, b)].astype(jnp.float32), blocks, out_ref)


def forward(table_ref, entries):
    return dot(table_ref[...], entries)


def backward(table_ref, real, imag):
    high, low = parts(jnp.concatenate([real, imag], axis=0))
    return dot(table_ref[...], jnp.concatenate([high, low], axis=0))


def polar_kernel(scale, entries_ref, own_ref, forward_ref, backward_ref, spectrum_ref, out_ref):
    spectrum = forward(forward_ref, entries_ref[...])
    spectrum_ref[...] = spectrum
    half, width = spectrum.shape[0] // 2, spectrum.shape[1] // 2
    edge = lax.broadcasted_iota(jnp.int32, (half, width), 0) == 0
    own = own_ref[...] > 0.5
    real = spectrum[:half, :width], spectrum[:half, width:]
    imag = spectrum[half:, :width], spectrum[half:, width:]
    for slot in range(2):
        mirror_real = jnp.where(own, real[slot], real[1 - slot])
        mirror_imag = jnp.where(own, imag[slot], imag[1 - slot])
        rr, ii = real[slot] * mirror_real, imag[slot] * mirror_imag
        ir, ri = imag[slot] * mirror_real, real[slot] * mirror_imag
        values = backward(backward_ref, jnp.where(edge, rr, rr + ii), jnp.where(edge, ii, ir - ri))
        out_ref[:, slot * width : (slot + 1) * width] = (values * scale).astype(jnp.bfloat16)


def screen_kernel(blocks, polar_ref, coulomb_ref, out_ref, matrix_ref, screened_ref):
    def store(a, b, value):
        matrix_ref[at(a, b)] = value.astype(jnp.bfloat16)

    unpack(polar_ref, blocks, store)
    coulomb = coulomb_ref[...]
    inner = dot(coulomb, matrix_ref[...]).astype(jnp.bfloat16)
    second = dot(inner, coulomb)
    third = dot(inner, second.astype(jnp.bfloat16))
    screened = (coulomb.astype(jnp.float32) + second + third).astype(jnp.bfloat16)
    screened_ref[...] = screened.astype(jnp.float32)
    pack(lambda a, b: screened_ref[at(a, b)], blocks, out_ref)


def sigma_kernel(scale, entries_ref, green_ref, forward_ref, backward_ref, out_ref):
    spectrum = forward(forward_ref, entries_ref[...])
    half = spectrum.shape[0] // 2
    edge = lax.broadcasted_iota(jnp.int32, (half, spectrum.shape[1]), 0) == 0
    real, imag = spectrum[:half], spectrum[half:]
    green_real, green_imag = green_ref[:half], green_ref[half:]
    rr, ii = green_real * real, green_imag * imag
    cross = green_real * imag + green_imag * real
    values = backward(backward_ref, jnp.where(edge, rr, rr - ii), jnp.where(edge, ii, cross))
    out_ref[...] = (values * scale).astype(jnp.bfloat16)


def final_kernel(blocks, inv_root, sigma_ref, green_ref, right_ref, left_ref, out_ref, total_ref):
    def store(a, b, value):
        if a == b == blocks - 1:
            value = value + right_ref[...]
        if a == b == 0:
            value = value + left_ref[...]
        total_ref[at(a, b)] = value.astype(jnp.bfloat16)

    unpack(sigma_ref, blocks, store)
    green = green_ref[...]
    dressed = dot(green, total_ref[...]).astype(jnp.bfloat16)
    updated = green.astype(jnp.float32) + dot(dressed, green) * inv_root
    out_ref[...] = updated.astype(jnp.bfloat16)


def call(kernel, outs, scratch=(), flops=0, moved=0):
    return pl.pallas_call(
        kernel,
        out_shape=outs,
        scratch_shapes=list(scratch),
        compiler_params=pltpu.CompilerParams(vmem_limit_bytes=LIMIT),
        cost_estimate=pl.CostEstimate(flops=flops, bytes_accessed=moved, transcendentals=0),
    )


def tables(energies):
    half = energies // 2

    def waves(shape, along):
        row = lax.broadcasted_iota(jnp.int32, shape, along)
        energy = lax.broadcasted_iota(jnp.int32, shape, 1 - along)
        frequency = row % half
        angle = ((frequency * energy) % energies).astype(jnp.float32) * (2.0 * math.pi / energies)
        nyquist = (1 - 2 * (energy % 2)).astype(jnp.float32)
        sine = jnp.where(frequency == 0, nyquist, -jnp.sin(angle))
        return jnp.where(row < half, jnp.cos(angle), sine), frequency == 0

    square = (energies, energies)
    ahead, _ = waves(square, 0)
    back, first = waves(square, 1)
    back = (back * (jnp.where(first, 1.0, 2.0) / energies)).astype(jnp.bfloat16)
    return ahead.astype(jnp.bfloat16), jnp.concatenate([back, back], axis=1)


def coupling_matrix(column_ids, coupling_values):
    width = column_ids.shape[0]
    hits = column_ids[:, :, None] == jnp.arange(width, dtype=jnp.int32)[None, None, :]
    summed = jnp.sum(
        jnp.where(hits, coupling_values.astype(jnp.float32)[:, :, None], jnp.float32(0.0)), axis=1
    )
    return summed.astype(jnp.bfloat16)


def from_behind(x, axis, by):
    size = lax.axis_size(axis)
    pairs = [(i, i + by) for i in range(size) if 0 <= i + by < size]
    return lax.ppermute(x, axis, pairs)


def exchange(x):
    return lax.all_to_all(x, "energy", split_axis=0, concat_axis=0, tiled=True)


def on_device(green_blocks, coulomb, couple_cols, couple_vals):
    green, coulomb_block = green_blocks[0, 0], coulomb[0]
    orbitals = green.shape[0]
    blocks = orbitals // BLOCK
    energies = lax.axis_size("energy")
    chunk = (energies, 2 * ROWS, BLOCK)
    flat = (energies, 2 * ROWS * BLOCK)
    f32, b16 = jnp.float32, jnp.bfloat16
    packed = call(functools.partial(pack_kernel, blocks), jax.ShapeDtypeStruct(chunk, b16))(green)
    packed, corners = lax.optimization_barrier((packed, green))
    entries = exchange(packed)

    ahead, back = tables(energies)
    owner = lax.axis_index("energy")
    column = jnp.arange(ROWS * BLOCK, dtype=jnp.int32)
    row = lax.rem(owner, OWNERS) * ROWS + column // BLOCK
    shares = owner >= energies - (blocks // 2) * OWNERS
    own = ((row == column % BLOCK) & shares).astype(f32)[None]

    interface = couple_cols.shape[1]
    last = orbitals - interface
    inv_root = 1.0 / math.sqrt(orbitals)
    coupling = coupling_matrix(couple_cols[0], couple_vals[0])
    next_corner = from_behind(corners[:interface, :interface], "slab", -1)
    near_prev = dot(coupling.T, corners[last:, last:]).astype(b16)
    left_part = from_behind((dot(near_prev, coupling) * inv_root).astype(b16), "slab", 1)
    near_next = dot(coupling, next_corner).astype(b16)
    right_part = dot(near_next, coupling.T) * inv_root
    entries, ahead, back, own, right_part, left_part = lax.optimization_barrier(
        (entries, ahead, back, own, right_part, left_part)
    )

    spectrum, polar = call(
        functools.partial(polar_kernel, 0.5 / math.sqrt(orbitals * energies)),
        (jax.ShapeDtypeStruct(flat, f32), jax.ShapeDtypeStruct(flat, b16)),
    )(entries.reshape(flat), own, ahead, back)
    polar = exchange(polar.reshape(chunk))

    screened = call(
        functools.partial(screen_kernel, blocks),
        jax.ShapeDtypeStruct(chunk, b16),
        (pltpu.VMEM((orbitals, orbitals), b16), pltpu.VMEM((orbitals, orbitals), f32)),
    )(polar, coulomb_block)
    screened = exchange(screened).reshape(flat)

    sigma = call(
        functools.partial(sigma_kernel, 0.2 / math.sqrt(energies)),
        jax.ShapeDtypeStruct(flat, b16),
    )(screened, spectrum, ahead, back)
    sigma = exchange(sigma.reshape(chunk))

    updated = call(
        functools.partial(final_kernel, blocks, inv_root),
        jax.ShapeDtypeStruct((orbitals, orbitals), b16),
        (pltpu.VMEM((orbitals, orbitals), b16),),
    )(sigma, green, right_part, left_part)
    return updated[None, None]


def solution(mesh):
    return jax.shard_map(
        on_device,
        mesh=mesh,
        in_specs=(
            P("energy", "slab", None, None),
            P("slab", None, None),
            P("slab", None, None),
            P("slab", None, None),
        ),
        out_specs=P("energy", "slab", None, None),
        check_vma=False,
    )
```

```python
import functools
import math

import jax
import jax.numpy as jnp
from jax import lax
from jax.experimental import pallas as pl
from jax.experimental.pallas import tpu as pltpu
from jax.sharding import PartitionSpec as P

BLOCK = 128
ROWS = 8
OWNERS = BLOCK // ROWS
LIMIT = 40 * 1024 * 1024


def pairs_of(blocks):
    apart = [(a, b) for a in range(blocks) for b in range(a + 1, blocks)]
    return apart, [(a, a + 1) for a in range(0, blocks, 2)]


def dot(left, right):
    return jnp.dot(left, right, preferred_element_type=jnp.float32)


def parts(values):
    high = values.astype(jnp.bfloat16)
    return high, (values - high.astype(jnp.float32)).astype(jnp.bfloat16)


def triangle():
    row = lax.broadcasted_iota(jnp.int32, (BLOCK, BLOCK), 0)
    column = lax.broadcasted_iota(jnp.int32, (BLOCK, BLOCK), 1)
    return row <= column, row < column


def pack(block, blocks, out_ref):
    apart, diagonal = pairs_of(blocks)
    upper, above = triangle()
    for p, (a, b) in enumerate(apart + diagonal):
        if p < len(apart):
            first, second = block(a, b), block(b, a).T
        else:
            one, two = block(a, a), block(b, b)
            first, second = jnp.where(upper, one, two), jnp.where(above, one.T, two.T)
        both = jnp.concatenate(
            [first.reshape(OWNERS, ROWS, BLOCK), second.reshape(OWNERS, ROWS, BLOCK)], axis=1
        )
        out_ref[p * OWNERS : (p + 1) * OWNERS] = both.astype(jnp.bfloat16)


def unpack(in_ref, blocks, store):
    apart, diagonal = pairs_of(blocks)
    upper, _ = triangle()
    for p, (a, b) in enumerate(apart + diagonal):
        both = in_ref[p * OWNERS : (p + 1) * OWNERS].astype(jnp.float32)
        first = both[:, :ROWS].reshape(BLOCK, BLOCK)
        second = both[:, ROWS:].reshape(BLOCK, BLOCK).T
        if p < len(apart):
            store(a, b, first)
            store(b, a, second)
        else:
            store(a, a, jnp.where(upper, first, second))
            store(b, b, jnp.where(upper, second, first))


def at(a, b):
    return pl.ds(a * BLOCK, BLOCK), pl.ds(b * BLOCK, BLOCK)


def pack_kernel(blocks, green_ref, out_ref):
    pack(lambda a, b: green_ref[at(a, b)].astype(jnp.float32), blocks, out_ref)


def flattened(entries_ref):
    energies, rows, width = entries_ref.shape
    return entries_ref[...].reshape(energies, rows * width)


def forward(table_ref, entries):
    return dot(table_ref[...], entries)


def backward(table_ref, real, imag):
    high, low = parts(jnp.concatenate([real, imag], axis=0))
    return dot(table_ref[...], jnp.concatenate([high, low], axis=0))


def polar_kernel(scale, entries_ref, own_ref, forward_ref, backward_ref, spectrum_ref, out_ref):
    spectrum = forward(forward_ref, flattened(entries_ref))
    spectrum_ref[...] = spectrum
    half, width = spectrum.shape[0] // 2, spectrum.shape[1] // 2
    edge = lax.broadcasted_iota(jnp.int32, (half, width), 0) == 0
    own = own_ref[...] > 0.5
    real = spectrum[:half, :width], spectrum[:half, width:]
    imag = spectrum[half:, :width], spectrum[half:, width:]
    values = []
    for slot in range(2):
        mirror_real = jnp.where(own, real[slot], real[1 - slot])
        mirror_imag = jnp.where(own, imag[slot], imag[1 - slot])
        rr, ii = real[slot] * mirror_real, imag[slot] * mirror_imag
        ir, ri = imag[slot] * mirror_real, real[slot] * mirror_imag
        values.append(
            backward(backward_ref, jnp.where(edge, rr, rr + ii), jnp.where(edge, ii, ir - ri))
        )
    both = (jnp.concatenate(values, axis=1) * scale).astype(jnp.bfloat16)
    out_ref[...] = both.reshape(out_ref.shape)


def screen_kernel(blocks, polar_ref, coulomb_ref, out_ref, matrix_ref, screened_ref):
    def store(a, b, value):
        matrix_ref[at(a, b)] = value.astype(jnp.bfloat16)

    unpack(polar_ref, blocks, store)
    coulomb = coulomb_ref[...]
    inner = dot(coulomb, matrix_ref[...]).astype(jnp.bfloat16)
    second = dot(inner, coulomb)
    third = dot(inner, second.astype(jnp.bfloat16))
    screened = (coulomb.astype(jnp.float32) + second + third).astype(jnp.bfloat16)
    screened_ref[...] = screened.astype(jnp.float32)
    pack(lambda a, b: screened_ref[at(a, b)], blocks, out_ref)


def sigma_kernel(scale, entries_ref, green_ref, forward_ref, backward_ref, out_ref):
    spectrum = forward(forward_ref, flattened(entries_ref))
    half = spectrum.shape[0] // 2
    edge = lax.broadcasted_iota(jnp.int32, (half, spectrum.shape[1]), 0) == 0
    real, imag = spectrum[:half], spectrum[half:]
    green_real, green_imag = green_ref[:half], green_ref[half:]
    rr, ii = green_real * real, green_imag * imag
    cross = green_real * imag + green_imag * real
    values = backward(backward_ref, jnp.where(edge, rr, rr - ii), jnp.where(edge, ii, cross))
    out_ref[...] = (values * scale).astype(jnp.bfloat16).reshape(out_ref.shape)


def final_kernel(blocks, inv_root, sigma_ref, green_ref, right_ref, left_ref, out_ref, total_ref):
    def store(a, b, value):
        if a == b == blocks - 1:
            value = value + right_ref[...]
        if a == b == 0:
            value = value + left_ref[...]
        total_ref[at(a, b)] = value.astype(jnp.bfloat16)

    unpack(sigma_ref, blocks, store)
    green = green_ref[...]
    dressed = dot(green, total_ref[...]).astype(jnp.bfloat16)
    updated = green.astype(jnp.float32) + dot(dressed, green) * inv_root
    out_ref[...] = updated.astype(jnp.bfloat16)


def call(kernel, outs, scratch=(), flops=0, moved=0):
    return pl.pallas_call(
        kernel,
        out_shape=outs,
        scratch_shapes=list(scratch),
        compiler_params=pltpu.CompilerParams(vmem_limit_bytes=LIMIT),
        cost_estimate=pl.CostEstimate(flops=flops, bytes_accessed=moved, transcendentals=0),
    )


def tables(energies):
    half = energies // 2

    def waves(shape, along):
        row = lax.broadcasted_iota(jnp.int32, shape, along)
        energy = lax.broadcasted_iota(jnp.int32, shape, 1 - along)
        frequency = row % half
        angle = ((frequency * energy) % energies).astype(jnp.float32) * (2.0 * math.pi / energies)
        nyquist = (1 - 2 * (energy % 2)).astype(jnp.float32)
        sine = jnp.where(frequency == 0, nyquist, -jnp.sin(angle))
        return jnp.where(row < half, jnp.cos(angle), sine), frequency == 0

    square = (energies, energies)
    ahead, _ = waves(square, 0)
    back, first = waves(square, 1)
    back = (back * (jnp.where(first, 1.0, 2.0) / energies)).astype(jnp.bfloat16)
    return ahead.astype(jnp.bfloat16), jnp.concatenate([back, back], axis=1)


def coupling_matrix(column_ids, coupling_values):
    width = column_ids.shape[0]
    hits = column_ids[:, :, None] == jnp.arange(width, dtype=jnp.int32)[None, None, :]
    summed = jnp.sum(
        jnp.where(hits, coupling_values.astype(jnp.float32)[:, :, None], jnp.float32(0.0)), axis=1
    )
    return summed.astype(jnp.bfloat16)


def from_behind(x, axis, by):
    size = lax.axis_size(axis)
    pairs = [(i, i + by) for i in range(size) if 0 <= i + by < size]
    return lax.ppermute(x, axis, pairs)


def exchange(x):
    return lax.all_to_all(x, "energy", split_axis=0, concat_axis=0, tiled=True)


def on_device(green_blocks, coulomb, couple_cols, couple_vals):
    green, coulomb_block = green_blocks[0, 0], coulomb[0]
    orbitals = green.shape[0]
    blocks = orbitals // BLOCK
    energies = lax.axis_size("energy")
    chunk = (energies, 2 * ROWS, BLOCK)
    flat = (energies, 2 * ROWS * BLOCK)
    f32, b16 = jnp.float32, jnp.bfloat16
    packed = call(functools.partial(pack_kernel, blocks), jax.ShapeDtypeStruct(chunk, b16))(green)
    packed, corners = lax.optimization_barrier((packed, green))
    entries = exchange(packed)

    ahead, back = tables(energies)
    owner = lax.axis_index("energy")
    column = jnp.arange(ROWS * BLOCK, dtype=jnp.int32)
    row = lax.rem(owner, OWNERS) * ROWS + column // BLOCK
    shares = owner >= energies - (blocks // 2) * OWNERS
    own = ((row == column % BLOCK) & shares).astype(f32)[None]

    interface = couple_cols.shape[1]
    last = orbitals - interface
    inv_root = 1.0 / math.sqrt(orbitals)
    coupling = coupling_matrix(couple_cols[0], couple_vals[0])
    behind = from_behind(jnp.concatenate([corners[last:, last:], coupling], axis=0), "slab", 1)
    prev_corner, previous = behind[:interface], behind[interface:]
    next_corner = from_behind(corners[:interface, :interface], "slab", -1)
    near_next = dot(coupling, next_corner).astype(b16)
    near_prev = dot(previous.T, prev_corner).astype(b16)
    right_part = dot(near_next, coupling.T) * inv_root
    left_part = dot(near_prev, previous) * inv_root
    entries, ahead, back, own, right_part, left_part = lax.optimization_barrier(
        (entries, ahead, back, own, right_part, left_part)
    )

    spectrum, polar = call(
        functools.partial(polar_kernel, 0.5 / math.sqrt(orbitals * energies)),
        (jax.ShapeDtypeStruct(flat, f32), jax.ShapeDtypeStruct(chunk, b16)),
    )(entries, own, ahead, back)
    polar = exchange(polar)

    screened = call(
        functools.partial(screen_kernel, blocks),
        jax.ShapeDtypeStruct(chunk, b16),
        (pltpu.VMEM((orbitals, orbitals), b16), pltpu.VMEM((orbitals, orbitals), f32)),
    )(polar, coulomb_block)
    screened = exchange(screened)

    sigma = call(
        functools.partial(sigma_kernel, 0.2 / math.sqrt(energies)),
        jax.ShapeDtypeStruct(chunk, b16),
    )(screened, spectrum, ahead, back)
    sigma = exchange(sigma)

    updated = call(
        functools.partial(final_kernel, blocks, inv_root),
        jax.ShapeDtypeStruct((orbitals, orbitals), b16),
        (pltpu.VMEM((orbitals, orbitals), b16),),
    )(sigma, green, right_part, left_part)
    return updated[None, None]


def solution(mesh):
    return jax.shard_map(
        on_device,
        mesh=mesh,
        in_specs=(
            P("energy", "slab", None, None),
            P("slab", None, None),
            P("slab", None, None),
            P("slab", None, None),
        ),
        out_specs=P("energy", "slab", None, None),
        check_vma=False,
    )
```

```python
import functools
import math

import jax
import jax.numpy as jnp
from jax import lax
from jax.experimental import pallas as pl
from jax.experimental.pallas import tpu as pltpu
from jax.sharding import PartitionSpec as P

BLOCK = 128
ROWS = 8
OWNERS = BLOCK // ROWS
LIMIT = 40 * 1024 * 1024


def pairs_of(blocks):
    apart = [(a, b) for a in range(blocks) for b in range(a + 1, blocks)]
    return apart, [(a, a + 1) for a in range(0, blocks, 2)]


def dot(left, right):
    return jnp.dot(left, right, preferred_element_type=jnp.float32)


def parts(values):
    high = values.astype(jnp.bfloat16)
    return high, (values - high.astype(jnp.float32)).astype(jnp.bfloat16)


def triangle():
    row = lax.broadcasted_iota(jnp.int32, (BLOCK, BLOCK), 0)
    column = lax.broadcasted_iota(jnp.int32, (BLOCK, BLOCK), 1)
    return row <= column, row < column


def pack(block, blocks, out_ref):
    apart, diagonal = pairs_of(blocks)
    upper, above = triangle()
    for p, (a, b) in enumerate(apart + diagonal):
        if p < len(apart):
            first, second = block(a, b), block(b, a).T
        else:
            one, two = block(a, a), block(b, b)
            first, second = jnp.where(upper, one, two), jnp.where(above, one.T, two.T)
        both = jnp.concatenate(
            [first.reshape(OWNERS, ROWS, BLOCK), second.reshape(OWNERS, ROWS, BLOCK)], axis=1
        )
        out_ref[p * OWNERS : (p + 1) * OWNERS] = both.astype(jnp.bfloat16)


def unpack(in_ref, blocks, store):
    apart, diagonal = pairs_of(blocks)
    upper, _ = triangle()
    for p, (a, b) in enumerate(apart + diagonal):
        both = in_ref[p * OWNERS : (p + 1) * OWNERS].astype(jnp.float32)
        first = both[:, :ROWS].reshape(BLOCK, BLOCK)
        second = both[:, ROWS:].reshape(BLOCK, BLOCK).T
        if p < len(apart):
            store(a, b, first)
            store(b, a, second)
        else:
            store(a, a, jnp.where(upper, first, second))
            store(b, b, jnp.where(upper, second, first))


def at(a, b):
    return pl.ds(a * BLOCK, BLOCK), pl.ds(b * BLOCK, BLOCK)


def pack_kernel(blocks, green_ref, out_ref):
    pack(lambda a, b: green_ref[at(a, b)].astype(jnp.float32), blocks, out_ref)


def flattened(entries_ref):
    energies, rows, width = entries_ref.shape
    return entries_ref[...].reshape(energies, rows * width)


def forward(table_ref, entries):
    return dot(table_ref[...], entries)


def backward(table_ref, real, imag):
    high, low = parts(jnp.concatenate([real, imag], axis=0))
    return dot(table_ref[...], jnp.concatenate([high, low], axis=0))


def polar_kernel(scale, entries_ref, own_ref, forward_ref, backward_ref, spectrum_ref, out_ref):
    spectrum = forward(forward_ref, flattened(entries_ref))
    spectrum_ref[...] = spectrum
    half, width = spectrum.shape[0] // 2, spectrum.shape[1] // 2
    edge = lax.broadcasted_iota(jnp.int32, (half, width), 0) == 0
    own = own_ref[...] > 0.5
    real = spectrum[:half, :width], spectrum[:half, width:]
    imag = spectrum[half:, :width], spectrum[half:, width:]
    values = []
    for slot in range(2):
        mirror_real = jnp.where(own, real[slot], real[1 - slot])
        mirror_imag = jnp.where(own, imag[slot], imag[1 - slot])
        rr, ii = real[slot] * mirror_real, imag[slot] * mirror_imag
        ir, ri = imag[slot] * mirror_real, real[slot] * mirror_imag
        values.append(
            backward(backward_ref, jnp.where(edge, rr, rr + ii), jnp.where(edge, ii, ir - ri))
        )
    both = (jnp.concatenate(values, axis=1) * scale).astype(jnp.bfloat16)
    out_ref[...] = both.reshape(out_ref.shape)


def screen_kernel(blocks, polar_ref, coulomb_ref, out_ref, matrix_ref, screened_ref):
    def store(a, b, value):
        matrix_ref[at(a, b)] = value.astype(jnp.bfloat16)

    unpack(polar_ref, blocks, store)
    coulomb = coulomb_ref[...]
    inner = dot(coulomb, matrix_ref[...]).astype(jnp.bfloat16)
    second = dot(inner, coulomb)
    third = dot(inner, second.astype(jnp.bfloat16))
    screened = (coulomb.astype(jnp.float32) + second + third).astype(jnp.bfloat16)
    screened_ref[...] = screened.astype(jnp.float32)
    pack(lambda a, b: screened_ref[at(a, b)], blocks, out_ref)


def sigma_kernel(scale, entries_ref, green_ref, forward_ref, backward_ref, out_ref):
    spectrum = forward(forward_ref, flattened(entries_ref))
    half = spectrum.shape[0] // 2
    edge = lax.broadcasted_iota(jnp.int32, (half, spectrum.shape[1]), 0) == 0
    real, imag = spectrum[:half], spectrum[half:]
    green_real, green_imag = green_ref[:half], green_ref[half:]
    rr, ii = green_real * real, green_imag * imag
    cross = green_real * imag + green_imag * real
    values = backward(backward_ref, jnp.where(edge, rr, rr - ii), jnp.where(edge, ii, cross))
    out_ref[...] = (values * scale).astype(jnp.bfloat16).reshape(out_ref.shape)


def final_kernel(blocks, inv_root, sigma_ref, green_ref, right_ref, left_ref, out_ref):
    total = [[None] * blocks for _ in range(blocks)]

    def store(a, b, value):
        if a == b == blocks - 1:
            value = value + right_ref[...]
        if a == b == 0:
            value = value + left_ref[...]
        total[a][b] = value.astype(jnp.bfloat16)

    unpack(sigma_ref, blocks, store)
    green = green_ref[...]
    whole = jnp.concatenate([jnp.concatenate(row, axis=1) for row in total], axis=0)
    dressed = dot(green, whole).astype(jnp.bfloat16)
    updated = green.astype(jnp.float32) + dot(dressed, green) * inv_root
    out_ref[...] = updated.astype(jnp.bfloat16)


def call(kernel, outs, scratch=(), flops=0, moved=0):
    return pl.pallas_call(
        kernel,
        out_shape=outs,
        scratch_shapes=list(scratch),
        compiler_params=pltpu.CompilerParams(vmem_limit_bytes=LIMIT),
        cost_estimate=pl.CostEstimate(flops=flops, bytes_accessed=moved, transcendentals=0),
    )


def tables(energies):
    half = energies // 2

    def waves(shape, along):
        row = lax.broadcasted_iota(jnp.int32, shape, along)
        energy = lax.broadcasted_iota(jnp.int32, shape, 1 - along)
        frequency = row % half
        angle = ((frequency * energy) % energies).astype(jnp.float32) * (2.0 * math.pi / energies)
        nyquist = (1 - 2 * (energy % 2)).astype(jnp.float32)
        sine = jnp.where(frequency == 0, nyquist, -jnp.sin(angle))
        return jnp.where(row < half, jnp.cos(angle), sine), frequency == 0

    square = (energies, energies)
    ahead, _ = waves(square, 0)
    back, first = waves(square, 1)
    back = (back * (jnp.where(first, 1.0, 2.0) / energies)).astype(jnp.bfloat16)
    return ahead.astype(jnp.bfloat16), jnp.concatenate([back, back], axis=1)


def coupling_matrix(column_ids, coupling_values):
    width = column_ids.shape[0]
    hits = column_ids[:, :, None] == jnp.arange(width, dtype=jnp.int32)[None, None, :]
    summed = jnp.sum(
        jnp.where(hits, coupling_values.astype(jnp.float32)[:, :, None], jnp.float32(0.0)), axis=1
    )
    return summed.astype(jnp.bfloat16)


def from_behind(x, axis, by):
    size = lax.axis_size(axis)
    pairs = [(i, i + by) for i in range(size) if 0 <= i + by < size]
    return lax.ppermute(x, axis, pairs)


def exchange(x):
    return lax.all_to_all(x, "energy", split_axis=0, concat_axis=0, tiled=True)


def on_device(green_blocks, coulomb, couple_cols, couple_vals):
    green, coulomb_block = green_blocks[0, 0], coulomb[0]
    orbitals = green.shape[0]
    blocks = orbitals // BLOCK
    energies = lax.axis_size("energy")
    chunk = (energies, 2 * ROWS, BLOCK)
    flat = (energies, 2 * ROWS * BLOCK)
    f32, b16 = jnp.float32, jnp.bfloat16
    packed = call(functools.partial(pack_kernel, blocks), jax.ShapeDtypeStruct(chunk, b16))(green)
    packed, corners = lax.optimization_barrier((packed, green))
    entries = exchange(packed)

    ahead, back = tables(energies)
    owner = lax.axis_index("energy")
    column = jnp.arange(ROWS * BLOCK, dtype=jnp.int32)
    row = lax.rem(owner, OWNERS) * ROWS + column // BLOCK
    shares = owner >= energies - (blocks // 2) * OWNERS
    own = ((row == column % BLOCK) & shares).astype(f32)[None]

    interface = couple_cols.shape[1]
    last = orbitals - interface
    inv_root = 1.0 / math.sqrt(orbitals)
    coupling = coupling_matrix(couple_cols[0], couple_vals[0])
    behind = from_behind(jnp.concatenate([corners[last:, last:], coupling], axis=0), "slab", 1)
    prev_corner, previous = behind[:interface], behind[interface:]
    next_corner = from_behind(corners[:interface, :interface], "slab", -1)
    near_next = dot(coupling, next_corner).astype(b16)
    near_prev = dot(previous.T, prev_corner).astype(b16)
    right_part = dot(near_next, coupling.T) * inv_root
    left_part = dot(near_prev, previous) * inv_root
    entries, ahead, back, own, right_part, left_part = lax.optimization_barrier(
        (entries, ahead, back, own, right_part, left_part)
    )

    spectrum, polar = call(
        functools.partial(polar_kernel, 0.5 / math.sqrt(orbitals * energies)),
        (jax.ShapeDtypeStruct(flat, f32), jax.ShapeDtypeStruct(chunk, b16)),
    )(entries, own, ahead, back)
    polar = exchange(polar)

    screened = call(
        functools.partial(screen_kernel, blocks),
        jax.ShapeDtypeStruct(chunk, b16),
        (pltpu.VMEM((orbitals, orbitals), b16), pltpu.VMEM((orbitals, orbitals), f32)),
    )(polar, coulomb_block)
    screened = exchange(screened)

    sigma = call(
        functools.partial(sigma_kernel, 0.2 / math.sqrt(energies)),
        jax.ShapeDtypeStruct(chunk, b16),
    )(screened, spectrum, ahead, back)
    sigma = exchange(sigma)

    updated = call(
        functools.partial(final_kernel, blocks, inv_root),
        jax.ShapeDtypeStruct((orbitals, orbitals), b16),
    )(sigma, green, right_part, left_part)
    return updated[None, None]


def solution(mesh):
    return jax.shard_map(
        on_device,
        mesh=mesh,
        in_specs=(
            P("energy", "slab", None, None),
            P("slab", None, None),
            P("slab", None, None),
            P("slab", None, None),
        ),
        out_specs=P("energy", "slab", None, None),
        check_vma=False,
    )
```

```python
import functools
import math

import jax
import jax.numpy as jnp
from jax import lax
from jax.experimental import pallas as pl
from jax.experimental.pallas import tpu as pltpu
from jax.sharding import PartitionSpec as P

BLOCK = 128
ROWS = 8
OWNERS = BLOCK // ROWS
LIMIT = 40 * 1024 * 1024


def pairs_of(blocks):
    apart = [(a, b) for a in range(blocks) for b in range(a + 1, blocks)]
    return apart, [(a, a + 1) for a in range(0, blocks, 2)]


def dot(left, right):
    return jnp.dot(left, right, preferred_element_type=jnp.float32)


def parts(values):
    high = values.astype(jnp.bfloat16)
    return high, (values - high.astype(jnp.float32)).astype(jnp.bfloat16)


def triangle():
    row = lax.broadcasted_iota(jnp.int32, (BLOCK, BLOCK), 0)
    column = lax.broadcasted_iota(jnp.int32, (BLOCK, BLOCK), 1)
    return row <= column, row < column


def pack(block, blocks, out_ref, after=lambda p: None):
    apart, diagonal = pairs_of(blocks)
    upper, above = triangle()
    for p, (a, b) in enumerate(apart + diagonal):
        if p < len(apart):
            first, second = block(a, b), block(b, a).T
        else:
            one, two = block(a, a), block(b, b)
            first, second = jnp.where(upper, one, two), jnp.where(above, one.T, two.T)
        both = jnp.concatenate(
            [first.reshape(OWNERS, ROWS, BLOCK), second.reshape(OWNERS, ROWS, BLOCK)], axis=1
        )
        out_ref[p * OWNERS : (p + 1) * OWNERS] = both.astype(jnp.bfloat16)
        after(p)


def unpack(in_ref, blocks, store):
    apart, diagonal = pairs_of(blocks)
    upper, _ = triangle()
    for p, (a, b) in enumerate(apart + diagonal):
        both = in_ref[p * OWNERS : (p + 1) * OWNERS].astype(jnp.float32)
        first = both[:, :ROWS].reshape(BLOCK, BLOCK)
        second = both[:, ROWS:].reshape(BLOCK, BLOCK).T
        if p < len(apart):
            store(a, b, first)
            store(b, a, second)
        else:
            store(a, a, jnp.where(upper, first, second))
            store(b, b, jnp.where(upper, second, first))


def at(a, b):
    return pl.ds(a * BLOCK, BLOCK), pl.ds(b * BLOCK, BLOCK)


def pack_kernel(blocks, green_ref, out_ref, packed_ref, sems):
    half = packed_ref.shape[0] // 2
    copies = [
        pltpu.make_async_copy(
            packed_ref.at[pl.ds(i * half, half)], out_ref.at[pl.ds(i * half, half)], sems.at[i]
        )
        for i in range(2)
    ]

    def after(p):
        if (p + 1) * OWNERS % half == 0:
            copies[p * OWNERS // half].start()

    pack(lambda a, b: green_ref[at(a, b)].astype(jnp.float32), blocks, packed_ref, after)
    for copy in copies:
        copy.wait()


def flattened(entries_ref):
    energies, rows, width = entries_ref.shape
    return entries_ref[...].reshape(energies, rows * width)


def forward(table_ref, entries):
    return dot(table_ref[...], entries)


def backward(table_ref, real, imag):
    high, low = parts(jnp.concatenate([real, imag], axis=0))
    return dot(table_ref[...], jnp.concatenate([high, low], axis=0))


def polar_kernel(scale, entries_ref, own_ref, forward_ref, backward_ref, spectrum_ref, out_ref):
    spectrum = forward(forward_ref, flattened(entries_ref))
    spectrum_ref[...] = spectrum
    half, width = spectrum.shape[0] // 2, spectrum.shape[1] // 2
    edge = lax.broadcasted_iota(jnp.int32, (half, width), 0) == 0
    own = own_ref[...] > 0.5
    real = spectrum[:half, :width], spectrum[:half, width:]
    imag = spectrum[half:, :width], spectrum[half:, width:]
    values = []
    for slot in range(2):
        mirror_real = jnp.where(own, real[slot], real[1 - slot])
        mirror_imag = jnp.where(own, imag[slot], imag[1 - slot])
        rr, ii = real[slot] * mirror_real, imag[slot] * mirror_imag
        ir, ri = imag[slot] * mirror_real, real[slot] * mirror_imag
        values.append(
            backward(backward_ref, jnp.where(edge, rr, rr + ii), jnp.where(edge, ii, ir - ri))
        )
    both = (jnp.concatenate(values, axis=1) * scale).astype(jnp.bfloat16)
    out_ref[...] = both.reshape(out_ref.shape)


def screen_kernel(blocks, polar_ref, coulomb_ref, out_ref, matrix_ref, screened_ref):
    def store(a, b, value):
        matrix_ref[at(a, b)] = value.astype(jnp.bfloat16)

    unpack(polar_ref, blocks, store)
    coulomb = coulomb_ref[...]
    inner = dot(coulomb, matrix_ref[...]).astype(jnp.bfloat16)
    second = dot(inner, coulomb)
    third = dot(inner, second.astype(jnp.bfloat16))
    screened = (coulomb.astype(jnp.float32) + second + third).astype(jnp.bfloat16)
    screened_ref[...] = screened.astype(jnp.float32)
    pack(lambda a, b: screened_ref[at(a, b)], blocks, out_ref)


def sigma_kernel(scale, entries_ref, green_ref, forward_ref, backward_ref, out_ref):
    spectrum = forward(forward_ref, flattened(entries_ref))
    half = spectrum.shape[0] // 2
    edge = lax.broadcasted_iota(jnp.int32, (half, spectrum.shape[1]), 0) == 0
    real, imag = spectrum[:half], spectrum[half:]
    green_real, green_imag = green_ref[:half], green_ref[half:]
    rr, ii = green_real * real, green_imag * imag
    cross = green_real * imag + green_imag * real
    values = backward(backward_ref, jnp.where(edge, rr, rr - ii), jnp.where(edge, ii, cross))
    out_ref[...] = (values * scale).astype(jnp.bfloat16).reshape(out_ref.shape)


def final_kernel(blocks, inv_root, sigma_ref, green_ref, right_ref, left_ref, out_ref):
    total = [[None] * blocks for _ in range(blocks)]

    def store(a, b, value):
        if a == b == blocks - 1:
            value = value + right_ref[...]
        if a == b == 0:
            value = value + left_ref[...]
        total[a][b] = value.astype(jnp.bfloat16)

    unpack(sigma_ref, blocks, store)
    green = green_ref[...]
    whole = jnp.concatenate([jnp.concatenate(row, axis=1) for row in total], axis=0)
    dressed = dot(green, whole).astype(jnp.bfloat16)
    updated = green.astype(jnp.float32) + dot(dressed, green) * inv_root
    out_ref[...] = updated.astype(jnp.bfloat16)


def call(kernel, outs, scratch=(), flops=0, moved=0, **specs):
    return pl.pallas_call(
        kernel,
        out_shape=outs,
        **specs,
        scratch_shapes=list(scratch),
        compiler_params=pltpu.CompilerParams(vmem_limit_bytes=LIMIT),
        cost_estimate=pl.CostEstimate(flops=flops, bytes_accessed=moved, transcendentals=0),
    )


def tables(energies):
    half = energies // 2

    def waves(shape, along):
        row = lax.broadcasted_iota(jnp.int32, shape, along)
        energy = lax.broadcasted_iota(jnp.int32, shape, 1 - along)
        frequency = row % half
        angle = ((frequency * energy) % energies).astype(jnp.float32) * (2.0 * math.pi / energies)
        nyquist = (1 - 2 * (energy % 2)).astype(jnp.float32)
        sine = jnp.where(frequency == 0, nyquist, -jnp.sin(angle))
        return jnp.where(row < half, jnp.cos(angle), sine), frequency == 0

    square = (energies, energies)
    ahead, _ = waves(square, 0)
    back, first = waves(square, 1)
    back = (back * (jnp.where(first, 1.0, 2.0) / energies)).astype(jnp.bfloat16)
    return ahead.astype(jnp.bfloat16), jnp.concatenate([back, back], axis=1)


def coupling_matrix(column_ids, coupling_values):
    width = column_ids.shape[0]
    hits = column_ids[:, :, None] == jnp.arange(width, dtype=jnp.int32)[None, None, :]
    summed = jnp.sum(
        jnp.where(hits, coupling_values.astype(jnp.float32)[:, :, None], jnp.float32(0.0)), axis=1
    )
    return summed.astype(jnp.bfloat16)


def from_behind(x, axis, by):
    size = lax.axis_size(axis)
    pairs = [(i, i + by) for i in range(size) if 0 <= i + by < size]
    return lax.ppermute(x, axis, pairs)


def exchange(x):
    return lax.all_to_all(x, "energy", split_axis=0, concat_axis=0, tiled=True)


def on_device(green_blocks, coulomb, couple_cols, couple_vals):
    green, coulomb_block = green_blocks[0, 0], coulomb[0]
    orbitals = green.shape[0]
    blocks = orbitals // BLOCK
    energies = lax.axis_size("energy")
    chunk = (energies, 2 * ROWS, BLOCK)
    flat = (energies, 2 * ROWS * BLOCK)
    f32, b16 = jnp.float32, jnp.bfloat16
    packed = call(
        functools.partial(pack_kernel, blocks),
        jax.ShapeDtypeStruct(chunk, b16),
        (pltpu.VMEM(chunk, b16), pltpu.SemaphoreType.DMA((2,))),
        out_specs=pl.BlockSpec(memory_space=pltpu.HBM),
    )(green)
    packed, corners = lax.optimization_barrier((packed, green))
    entries = exchange(packed)

    ahead, back = tables(energies)
    owner = lax.axis_index("energy")
    column = jnp.arange(ROWS * BLOCK, dtype=jnp.int32)
    row = lax.rem(owner, OWNERS) * ROWS + column // BLOCK
    shares = owner >= energies - (blocks // 2) * OWNERS
    own = ((row == column % BLOCK) & shares).astype(f32)[None]

    interface = couple_cols.shape[1]
    last = orbitals - interface
    inv_root = 1.0 / math.sqrt(orbitals)
    coupling = coupling_matrix(couple_cols[0], couple_vals[0])
    behind = from_behind(jnp.concatenate([corners[last:, last:], coupling], axis=0), "slab", 1)
    prev_corner, previous = behind[:interface], behind[interface:]
    next_corner = from_behind(corners[:interface, :interface], "slab", -1)
    near_next = dot(coupling, next_corner).astype(b16)
    near_prev = dot(previous.T, prev_corner).astype(b16)
    right_part = dot(near_next, coupling.T) * inv_root
    left_part = dot(near_prev, previous) * inv_root
    entries, ahead, back, own, right_part, left_part = lax.optimization_barrier(
        (entries, ahead, back, own, right_part, left_part)
    )

    spectrum, polar = call(
        functools.partial(polar_kernel, 0.5 / math.sqrt(orbitals * energies)),
        (jax.ShapeDtypeStruct(flat, f32), jax.ShapeDtypeStruct(chunk, b16)),
    )(entries, own, ahead, back)
    polar = exchange(polar)

    screened = call(
        functools.partial(screen_kernel, blocks),
        jax.ShapeDtypeStruct(chunk, b16),
        (pltpu.VMEM((orbitals, orbitals), b16), pltpu.VMEM((orbitals, orbitals), f32)),
    )(polar, coulomb_block)
    screened = exchange(screened)

    sigma = call(
        functools.partial(sigma_kernel, 0.2 / math.sqrt(energies)),
        jax.ShapeDtypeStruct(chunk, b16),
    )(screened, spectrum, ahead, back)
    sigma = exchange(sigma)

    updated = call(
        functools.partial(final_kernel, blocks, inv_root),
        jax.ShapeDtypeStruct((orbitals, orbitals), b16),
    )(sigma, green, right_part, left_part)
    return updated[None, None]


def solution(mesh):
    return jax.shard_map(
        on_device,
        mesh=mesh,
        in_specs=(
            P("energy", "slab", None, None),
            P("slab", None, None),
            P("slab", None, None),
            P("slab", None, None),
        ),
        out_specs=P("energy", "slab", None, None),
        check_vma=False,
    )
```

```python
import functools
import math

import jax
import jax.numpy as jnp
from jax import lax
from jax.experimental import pallas as pl
from jax.experimental.pallas import tpu as pltpu
from jax.sharding import PartitionSpec as P

BLOCK = 128
ROWS = 8
OWNERS = BLOCK // ROWS
LIMIT = 40 * 1024 * 1024


def pairs_of(blocks):
    apart = [(a, b) for a in range(blocks) for b in range(a + 1, blocks)]
    return apart, [(a, a + 1) for a in range(0, blocks, 2)]


def dot(left, right):
    return jnp.dot(left, right, preferred_element_type=jnp.float32)


def parts(values):
    high = values.astype(jnp.bfloat16)
    return high, (values - high.astype(jnp.float32)).astype(jnp.bfloat16)


def triangle():
    row = lax.broadcasted_iota(jnp.int32, (BLOCK, BLOCK), 0)
    column = lax.broadcasted_iota(jnp.int32, (BLOCK, BLOCK), 1)
    return row <= column, row < column


def pack(block, blocks, out_ref):
    apart, diagonal = pairs_of(blocks)
    upper, above = triangle()
    for p, (a, b) in enumerate(apart + diagonal):
        if p < len(apart):
            first, second = block(a, b), block(b, a).T
        else:
            one, two = block(a, a), block(b, b)
            first, second = jnp.where(upper, one, two), jnp.where(above, one.T, two.T)
        both = jnp.concatenate(
            [first.reshape(OWNERS, ROWS, BLOCK), second.reshape(OWNERS, ROWS, BLOCK)], axis=1
        )
        out_ref[p * OWNERS : (p + 1) * OWNERS] = both.astype(jnp.bfloat16)


def unpack(in_ref, blocks, store):
    apart, diagonal = pairs_of(blocks)
    upper, _ = triangle()
    for p, (a, b) in enumerate(apart + diagonal):
        both = in_ref[p * OWNERS : (p + 1) * OWNERS].astype(jnp.float32)
        first = both[:, :ROWS].reshape(BLOCK, BLOCK)
        second = both[:, ROWS:].reshape(BLOCK, BLOCK).T
        if p < len(apart):
            store(a, b, first)
            store(b, a, second)
        else:
            store(a, a, jnp.where(upper, first, second))
            store(b, b, jnp.where(upper, second, first))


def at(a, b):
    return pl.ds(a * BLOCK, BLOCK), pl.ds(b * BLOCK, BLOCK)


def pack_kernel(blocks, green_ref, out_ref):
    pack(lambda a, b: green_ref[at(a, b)].astype(jnp.float32), blocks, out_ref)


def flattened(entries_ref):
    energies, rows, width = entries_ref.shape
    return entries_ref[...].reshape(energies, rows * width)


def forward(table_ref, entries):
    return dot(table_ref[...], entries)


def backward(table_ref, real, imag):
    high, low = parts(jnp.concatenate([real, imag], axis=0))
    return dot(table_ref[...], jnp.concatenate([high, low], axis=0))


def polar_kernel(scale, entries_ref, own_ref, forward_ref, backward_ref, spectrum_ref, out_ref):
    spectrum = forward(forward_ref, flattened(entries_ref))
    spectrum_ref[...] = spectrum
    half, width = spectrum.shape[0] // 2, spectrum.shape[1] // 2
    edge = lax.broadcasted_iota(jnp.int32, (half, width), 0) == 0
    own = own_ref[...] > 0.5
    real = spectrum[:half, :width], spectrum[:half, width:]
    imag = spectrum[half:, :width], spectrum[half:, width:]
    values = []
    for slot in range(2):
        mirror_real = jnp.where(own, real[slot], real[1 - slot])
        mirror_imag = jnp.where(own, imag[slot], imag[1 - slot])
        rr, ii = real[slot] * mirror_real, imag[slot] * mirror_imag
        ir, ri = imag[slot] * mirror_real, real[slot] * mirror_imag
        values.append(
            backward(backward_ref, jnp.where(edge, rr, rr + ii), jnp.where(edge, ii, ir - ri))
        )
    both = (jnp.concatenate(values, axis=1) * scale).astype(jnp.bfloat16)
    out_ref[...] = both.reshape(out_ref.shape)


def screen_kernel(blocks, polar_ref, coulomb_ref, out_ref, matrix_ref):
    def store(a, b, value):
        matrix_ref[at(a, b)] = value.astype(jnp.bfloat16)

    unpack(polar_ref, blocks, store)
    coulomb = coulomb_ref[...]
    inner = dot(coulomb, matrix_ref[...]).astype(jnp.bfloat16)
    half = coulomb.shape[1] // 2
    sides = [slice(0, half), slice(half, 2 * half)]
    second = [dot(inner, coulomb_ref[:, side]) for side in sides]
    rounded = [part.astype(jnp.bfloat16) for part in second]
    screened = jnp.concatenate(
        [
            coulomb_ref[:, side].astype(jnp.float32) + part + dot(inner, low)
            for side, part, low in zip(sides, second, rounded)
        ],
        axis=1,
    )

    def block(a, b):
        return screened[a * BLOCK : (a + 1) * BLOCK, b * BLOCK : (b + 1) * BLOCK]

    pack(block, blocks, out_ref)


def sigma_kernel(scale, entries_ref, green_ref, forward_ref, backward_ref, out_ref):
    spectrum = forward(forward_ref, flattened(entries_ref))
    half = spectrum.shape[0] // 2
    edge = lax.broadcasted_iota(jnp.int32, (half, spectrum.shape[1]), 0) == 0
    real, imag = spectrum[:half], spectrum[half:]
    green_real, green_imag = green_ref[:half], green_ref[half:]
    rr, ii = green_real * real, green_imag * imag
    cross = green_real * imag + green_imag * real
    values = backward(backward_ref, jnp.where(edge, rr, rr - ii), jnp.where(edge, ii, cross))
    out_ref[...] = (values * scale).astype(jnp.bfloat16).reshape(out_ref.shape)


def final_kernel(blocks, inv_root, sigma_ref, green_ref, right_ref, left_ref, out_ref):
    total = [[None] * blocks for _ in range(blocks)]

    def store(a, b, value):
        if a == b == blocks - 1:
            value = value + right_ref[...]
        if a == b == 0:
            value = value + left_ref[...]
        total[a][b] = value.astype(jnp.bfloat16)

    unpack(sigma_ref, blocks, store)
    green = green_ref[...]
    whole = jnp.concatenate([jnp.concatenate(row, axis=1) for row in total], axis=0)
    dressed = dot(green, whole).astype(jnp.bfloat16)
    updated = green.astype(jnp.float32) + dot(dressed, green) * inv_root
    out_ref[...] = updated.astype(jnp.bfloat16)


def call(kernel, outs, scratch=(), flops=0, moved=0):
    return pl.pallas_call(
        kernel,
        out_shape=outs,
        scratch_shapes=list(scratch),
        compiler_params=pltpu.CompilerParams(vmem_limit_bytes=LIMIT),
        cost_estimate=pl.CostEstimate(flops=flops, bytes_accessed=moved, transcendentals=0),
    )


def tables(energies):
    half = energies // 2

    def waves(shape, along):
        row = lax.broadcasted_iota(jnp.int32, shape, along)
        energy = lax.broadcasted_iota(jnp.int32, shape, 1 - along)
        frequency = row % half
        angle = ((frequency * energy) % energies).astype(jnp.float32) * (2.0 * math.pi / energies)
        nyquist = (1 - 2 * (energy % 2)).astype(jnp.float32)
        sine = jnp.where(frequency == 0, nyquist, -jnp.sin(angle))
        return jnp.where(row < half, jnp.cos(angle), sine), frequency == 0

    square = (energies, energies)
    ahead, _ = waves(square, 0)
    back, first = waves(square, 1)
    back = (back * (jnp.where(first, 1.0, 2.0) / energies)).astype(jnp.bfloat16)
    return ahead.astype(jnp.bfloat16), jnp.concatenate([back, back], axis=1)


def coupling_matrix(column_ids, coupling_values):
    width = column_ids.shape[0]
    hits = column_ids[:, :, None] == jnp.arange(width, dtype=jnp.int32)[None, None, :]
    summed = jnp.sum(
        jnp.where(hits, coupling_values.astype(jnp.float32)[:, :, None], jnp.float32(0.0)), axis=1
    )
    return summed.astype(jnp.bfloat16)


def from_behind(x, axis, by):
    size = lax.axis_size(axis)
    pairs = [(i, i + by) for i in range(size) if 0 <= i + by < size]
    return lax.ppermute(x, axis, pairs)


def exchange(x):
    return lax.all_to_all(x, "energy", split_axis=0, concat_axis=0, tiled=True)


def on_device(green_blocks, coulomb, couple_cols, couple_vals):
    green, coulomb_block = green_blocks[0, 0], coulomb[0]
    orbitals = green.shape[0]
    blocks = orbitals // BLOCK
    energies = lax.axis_size("energy")
    chunk = (energies, 2 * ROWS, BLOCK)
    flat = (energies, 2 * ROWS * BLOCK)
    f32, b16 = jnp.float32, jnp.bfloat16
    packed = call(functools.partial(pack_kernel, blocks), jax.ShapeDtypeStruct(chunk, b16))(green)
    packed, corners = lax.optimization_barrier((packed, green))
    entries = exchange(packed)

    ahead, back = tables(energies)
    owner = lax.axis_index("energy")
    column = jnp.arange(ROWS * BLOCK, dtype=jnp.int32)
    row = lax.rem(owner, OWNERS) * ROWS + column // BLOCK
    shares = owner >= energies - (blocks // 2) * OWNERS
    own = ((row == column % BLOCK) & shares).astype(f32)[None]

    interface = couple_cols.shape[1]
    last = orbitals - interface
    inv_root = 1.0 / math.sqrt(orbitals)
    coupling = coupling_matrix(couple_cols[0], couple_vals[0])
    behind = from_behind(jnp.concatenate([corners[last:, last:], coupling], axis=0), "slab", 1)
    prev_corner, previous = behind[:interface], behind[interface:]
    next_corner = from_behind(corners[:interface, :interface], "slab", -1)
    near_next = dot(coupling, next_corner).astype(b16)
    near_prev = dot(previous.T, prev_corner).astype(b16)
    right_part = dot(near_next, coupling.T) * inv_root
    left_part = dot(near_prev, previous) * inv_root
    entries, ahead, back, own, right_part, left_part = lax.optimization_barrier(
        (entries, ahead, back, own, right_part, left_part)
    )

    spectrum, polar = call(
        functools.partial(polar_kernel, 0.5 / math.sqrt(orbitals * energies)),
        (jax.ShapeDtypeStruct(flat, f32), jax.ShapeDtypeStruct(chunk, b16)),
    )(entries, own, ahead, back)
    polar = exchange(polar)

    screened = call(
        functools.partial(screen_kernel, blocks),
        jax.ShapeDtypeStruct(chunk, b16),
        (pltpu.VMEM((orbitals, orbitals), b16),),
    )(polar, coulomb_block)
    screened = exchange(screened)

    sigma = call(
        functools.partial(sigma_kernel, 0.2 / math.sqrt(energies)),
        jax.ShapeDtypeStruct(chunk, b16),
    )(screened, spectrum, ahead, back)
    sigma = exchange(sigma)

    updated = call(
        functools.partial(final_kernel, blocks, inv_root),
        jax.ShapeDtypeStruct((orbitals, orbitals), b16),
    )(sigma, green, right_part, left_part)
    return updated[None, None]


def solution(mesh):
    return jax.shard_map(
        on_device,
        mesh=mesh,
        in_specs=(
            P("energy", "slab", None, None),
            P("slab", None, None),
            P("slab", None, None),
            P("slab", None, None),
        ),
        out_specs=P("energy", "slab", None, None),
        check_vma=False,
    )
```
